512 devices in a mesh: blk: 256 (over y, x_lo, z, core), rep: 2 (over x_hi).
Axes of the slice: x: 4 (x_hi: 2, x_lo: 2; x = x_hi * 2 + x_lo), y: 4, z: 16, core: 2. Of those that a mesh axis runs over, the one named last changes fastest.
Arguments:
- images: bfloat16 [2, 98304, 1024], P('rep', 'blk'), may hold values from -27 to 27
- texts: bfloat16 [2, 98304, 1024], P('rep', 'blk'), may hold values from -27 to 27
- log_scale: float32 [], replicated, may hold values from -2.6 to -2
Outputs:
- grad_image: bfloat16 [2, 98304, 1024], P('rep', 'blk')
- grad_text: bfloat16 [2, 98304, 1024], P('rep', 'blk')
- loss: float32 [], replicated
- grad_scale: float32 [], replicated
The draws below stay inside these ranges and needn't reach their ends.
All inputs are finite; a program needn't handle non-finite values.
Results may differ from the reference program's by a relative error of at most 0.0041.
Values may be sent and summed in bfloat16 or wider, within the bound.
A program may use at most 64 MiB of HBM per device.

```python
import jax
import jax.numpy as jnp
from jax import lax

E = 1024
R_DEV = 384
HOPS = 4
REPS = 2
ROWS = 98304
N_BLK = 256


def shared_noise(key):
    return jnp.clip(jax.random.normal(key, (REPS, ROWS, E), jnp.float32), -6.0, 6.0)


def block_factors(key):
    blocks = ROWS // R_DEV
    slope_part = jnp.arange(blocks, dtype=jnp.float32) / max(blocks - 1, 1)
    jitter = jax.random.uniform(key, (REPS, blocks), jnp.float32, 0.0, jnp.log(1.4))
    levels = jnp.exp(jnp.log(0.55) + 0.5 * jnp.log(2.0) * slope_part[None, :] + jitter)
    group_scale = jnp.where(jnp.arange(REPS) % 2 == 1, 0.55, 1.0).astype(jnp.float32)
    factors = levels * group_scale[:, None]
    return jnp.repeat(factors, R_DEV, axis=1)[:, :, None]


def draw_images(key, part):
    base = shared_noise(key)
    key = jax.random.fold_in(key, 3)
    base = base * block_factors(jax.random.fold_in(key, 11))
    return base.astype(jnp.bfloat16)


def draw_texts(key, part):
    base = shared_noise(key)
    key = jax.random.fold_in(key, 7)
    own = jnp.clip(jax.random.normal(key, (REPS, ROWS, E), jnp.float32), -6.0, 6.0)
    mixed = 0.1 * base + 0.995 * own
    return mixed.astype(jnp.bfloat16)


def setup_inputs(seed: int = 0) -> dict:
    streams_of = jax.random.split(jax.random.key(seed), 4)
    return {
        "images": draw_images(jax.random.fold_in(streams_of[3], 71), 0),
        "texts": draw_texts(jax.random.fold_in(streams_of[3], 71), 0),
        "log_scale": jnp.clip(jax.random.uniform(streams_of[2], (), jnp.float32, -2.6, -2.0), -2.6, -2.0),
    }


def lse_rows(tile):
    return jax.nn.logsumexp(tile, axis=1)


def lse_cols(tile):
    return jax.nn.logsumexp(tile, axis=0)


def one_group(image_group, text_group, scale):
    image_blocks = image_group.reshape(N_BLK, R_DEV, E)
    text_blocks = text_group.reshape(N_BLK, R_DEV, E)
    diagonal = scale * jnp.sum(image_blocks.astype(jnp.float32) * text_blocks.astype(jnp.float32), axis=-1)
    row_lse = None
    col_lse = None
    for offset in range(HOPS + 1):
        moved = jnp.roll(text_blocks, offset, axis=0)

        def tile_stats(pair):
            logits = scale * jnp.dot(pair[0], pair[1].T, preferred_element_type=jnp.float32)
            return lse_rows(logits), lse_cols(logits)

        row_part, col_part = lax.map(tile_stats, (image_blocks, moved))
        col_part = jnp.roll(col_part, -offset, axis=0)
        row_lse = row_part if row_lse is None else jnp.logaddexp(row_lse, row_part)
        col_lse = col_part if col_lse is None else jnp.logaddexp(col_lse, col_part)
    image_acc = jnp.zeros((N_BLK, R_DEV, E), jnp.float32)
    text_acc = jnp.zeros((N_BLK, R_DEV, E), jnp.float32)
    scale_acc = jnp.zeros((), jnp.float32)
    identity = jnp.eye(R_DEV, dtype=jnp.float32)
    for offset in range(HOPS + 1):
        moved = jnp.roll(text_blocks, offset, axis=0)
        col_moved = jnp.roll(col_lse, offset, axis=0)
        is_diag = offset == 0

        def grad_tile(items):
            image_rows, text_rows, row_vals, col_vals = items
            logits = scale * jnp.dot(image_rows, text_rows.T, preferred_element_type=jnp.float32)
            weights = 0.5 * (jnp.exp(logits - row_vals[:, None]) + jnp.exp(logits - col_vals[None, :]))
            if is_diag:
                weights = weights - identity
            rounded = weights.astype(jnp.bfloat16)
            image_part = jnp.dot(rounded, text_rows, preferred_element_type=jnp.float32)
            text_part = jnp.dot(rounded.T, image_rows, preferred_element_type=jnp.float32)
            return image_part, text_part, jnp.sum(weights * logits)

        image_part, text_part, scale_part = lax.map(grad_tile, (image_blocks, moved, row_lse, col_moved))
        image_acc = image_acc + image_part
        text_acc = text_acc + jnp.roll(text_part, -offset, axis=0)
        scale_acc = scale_acc + jnp.sum(scale_part)
    loss_sum = jnp.sum(row_lse - diagonal) + jnp.sum(col_lse - diagonal)
    grad_img = (scale * image_acc).astype(jnp.bfloat16).reshape(ROWS, E)
    grad_txt = (scale * text_acc).astype(jnp.bfloat16).reshape(ROWS, E)
    return grad_img, grad_txt, loss_sum, scale_acc


def reference(images, texts, log_scale):
    scale = jnp.exp(log_scale.astype(jnp.float32))
    image_grads = []
    text_grads = []
    loss_total = jnp.zeros((), jnp.float32)
    scale_total = jnp.zeros((), jnp.float32)
    for group in range(REPS):
        grad_img, grad_txt, loss_sum, scale_sum = one_group(images[group], texts[group], scale)
        image_grads.append(grad_img)
        text_grads.append(grad_txt)
        loss_total = loss_total + loss_sum
        scale_total = scale_total + scale_sum
    count = REPS * ROWS
    return (jnp.stack(image_grads), jnp.stack(text_grads), 0.5 * loss_total / count, scale_total / count)
```

```python
import functools
import math

import jax
import jax.numpy as jnp
from jax import lax
from jax.experimental import pallas as pl
from jax.experimental.pallas import tpu as pltpu
from jax.sharding import PartitionSpec as P

HOPS = 4
KEYS = HOPS + 1
LOG2E = math.log2(math.e)
LN2 = math.log(2.0)
MESH = pl.DeviceIdType.MESH
PARTS = 3


def kernel(peers, ls_ref, img, txt, gimg, gtxt, loss, gscale,
           X, S, E, G, M, L, W, own_lse, LR, AR, lsem, ssem, rsem, lse_ssem, lse_rsem, ar_ssem, ar_rsem):
    rows = img.shape[1]
    width = img.shape[2]
    piece = rows // PARTS
    b = lax.axis_index("blk")
    rep = lax.axis_index("rep")
    core = lax.rem(b, 2)
    sib = b + 1 - 2 * core
    step = tuple(lax.rem(b + d + peers, peers) for d in (2, -2))
    own = (txt, img)

    low, mid, high = lax.rem(b, 8), lax.rem(b // 8, 8), lax.rem(b // 64, 4) * 2 + rep
    where = (low, mid, high)

    def group_peer(stage, m):
        at = lax.rem(where[stage] + m, 8)
        if stage == 0:
            return (b - low + at, rep)
        if stage == 1:
            return (b + 8 * (at - mid), rep)
        return (lax.rem(b, 64) + 64 * (at // 2), lax.rem(at, 2))

    barrier = pltpu.get_barrier_semaphore()
    near = [lax.rem(b + d + peers, peers) for d in (2, -2, 1, -1, 3, -3, 4, -4)]
    for d in near:
        pl.semaphore_signal(barrier, inc=1, device_id=(d, rep), device_id_type=MESH)
    for stage in range(3):
        for m in range(1, 8):
            pl.semaphore_signal(barrier, inc=1, device_id=group_peer(stage, m), device_id_type=MESH)
    loads = [pltpu.make_async_copy(own[p].at[0], X.at[p, pl.ds(0, rows)], lsem.at[p]) for p in range(2)]
    for load in loads:
        load.start()
    pl.semaphore_wait(barrier, len(near) + 21)

    sends = []

    def send(src, dst, s, r, d):
        copy = pltpu.make_async_remote_copy(
            src_ref=src, dst_ref=dst, send_sem=s, recv_sem=r, device_id=d, device_id_type=MESH)
        copy.start()
        sends.append(copy)

    def at(k, j):
        return pl.ds(rows * k + j * piece, piece)

    def arrived(p, k, j):
        here = X.at[p, at(k, j)]
        pltpu.make_async_remote_copy(
            src_ref=here, dst_ref=here, send_sem=ssem.at[0, 0, 0], recv_sem=rsem.at[p, k, j],
            device_id=(sib, rep), device_id_type=MESH).wait_recv()

    for j in range(PARTS):
        for p in range(2):
            send(own[p].at[0, pl.ds(j * piece, piece)], X.at[p, at(2, j)], ssem.at[0, p, j], rsem.at[p, 2, j], (step[p], rep))
    for load in loads:
        load.wait()
    for j in range(PARTS):
        send(X.at[core, at(0, j)], X.at[core, at(1, j)], ssem.at[1, 0, j], rsem.at[core, 1, j], (sib, rep))

    scale = jnp.exp(jnp.full((1, 1), ls_ref[0], jnp.float32))
    scale2 = scale * LOG2E

    def score(p, first, count, start=False):
        s = scale2 * lax.dot_general(
            X[1 - p, pl.ds(0, rows)], X[p, pl.ds(first, count)], (((1,), (1,)), ((), ())),
            preferred_element_type=jnp.float32)
        S[p, :, pl.ds(first, count)] = s
        top = jnp.max(s, axis=1, keepdims=True)
        if not start:
            old = M[p]
            top = jnp.maximum(top, old)
        e = jnp.exp2(s - top)
        total = jnp.sum(e, axis=1, keepdims=True)
        weighted = jnp.sum(e * s, axis=1, keepdims=True)
        if not start:
            fade = jnp.exp2(old - top)
            total = total + fade * L[p]
            weighted = weighted + fade * W[p]
        M[p], L[p], W[p] = top, total, weighted
        return s

    eye = (lax.broadcasted_iota(jnp.int32, (rows, rows), 0) == lax.broadcasted_iota(jnp.int32, (rows, rows), 1))
    tile = score(0, 0, rows, start=True)
    diag = jnp.sum(jnp.where(eye, tile, 0.0))
    score(1, 0, rows, start=True)

    for j in range(PARTS):
        for p in range(2):
            arrived(p, 2, j)
            send(X.at[p, at(2, j)], X.at[p, at(4, j)], ssem.at[2, p, j], rsem.at[p, 4, j], (step[p], rep))
            k = 3 - 2 * core if p == 0 else 1 + 2 * core
            send(X.at[p, at(2, j)], X.at[p, at(k, j)], ssem.at[3, p, j], rsem.at[p, k, j], (sib, rep))
    for p in range(2):
        score(p, 2 * rows, rows)
    for p in range(2):
        for j in range(PARTS):
            arrived(p, 1, j)
        score(p, rows, rows)
    for j in range(PARTS):
        arrived(1 - core, 3, j)
    score(1 - core, 3 * rows, rows)
    for j in range(PARTS):
        arrived(1 - core, 4, j)
        send(X.at[1 - core, at(4, j)], X.at[1 - core, at(3, j)], ssem.at[1, 1, j], rsem.at[1 - core, 3, j], (sib, rep))
        arrived(core, 4, j)
        for p in range(2):
            score(p, 4 * rows + j * piece, piece)
        arrived(core, 3, j)
        score(core, 3 * rows + j * piece, piece)

    for p in range(2):
        half = M[p] + jnp.log2(L[p]) + 1.0
        M[p] = half
        flat = jnp.broadcast_to(half, (rows, 128)).T[0:8]
        own_lse[p] = flat
        LR[1 - p, :, pl.ds(0, rows)] = flat
        for k in range(1, KEYS):
            there = lax.rem(b + (k if p == 1 else peers - k), peers)
            send(own_lse.at[p], LR.at[1 - p, :, pl.ds(k * rows, rows)], lse_ssem.at[p, k], lse_rsem.at[1 - p, k], (there, rep))

    lse_sum = jnp.sum(M[0] + M[1]) - 2.0 * rows
    pull = jnp.sum(W[0] / L[0] + W[1] / L[1])
    local_loss = lse_sum - 2.0 * diag
    local_scale = 0.5 * pull - diag
    top_row = lax.broadcasted_iota(jnp.int32, (8, 128), 0) == 0
    part = jnp.where(top_row, local_loss, local_scale)

    def share(stage, value):
        mine = AR.at[stage, where[stage]]
        mine[...] = value
        for m in range(1, 8):
            send(mine, mine, ar_ssem.at[stage, m], ar_rsem.at[stage], group_peer(stage, m))

    def gather(stage):
        seven = AR.at[stage, pl.ds(0, 7)]
        pltpu.make_async_remote_copy(
            src_ref=seven, dst_ref=seven, send_sem=ar_ssem.at[stage, 0], recv_sem=ar_rsem.at[stage],
            device_id=(sib, rep), device_id_type=MESH).wait_recv()
        total = AR[stage, 0]
        for i in range(1, 8):
            total = total + AR[stage, i]
        return total

    share(0, part)
    for p in range(2):
        E[p] = jnp.exp2(S[p] - M[p])
    share(1, gather(0))

    out = (gimg, gtxt)
    for p in range(2):
        for k in range(1, KEYS):
            here = LR.at[p, :, pl.ds(k * rows, rows)]
            pltpu.make_async_remote_copy(
                src_ref=here, dst_ref=here, send_sem=lse_ssem.at[p, 0], recv_sem=lse_rsem.at[p, k],
                device_id=(sib, rep), device_id_type=MESH).wait_recv()
        for k in range(KEYS):
            cols = pl.ds(k * rows, rows)
            g = E[p, :, cols] + jnp.exp2(S[p, :, cols] - LR[p, 0:1, cols])
            if k == 0:
                g = g - eye.astype(jnp.float32)
            G[p, :, cols] = g.astype(jnp.bfloat16)
        for n in range(0, width, 256):
            acc = jnp.dot(G[p], X[p, :, pl.ds(n, 256)], preferred_element_type=jnp.float32)
            out[p][0, :, pl.ds(n, 256)] = (scale * acc).astype(jnp.bfloat16)
        if p == 0:
            share(2, gather(1))
    total = gather(2) * (LN2 / (2 * peers * rows))
    loss[0] = 0.5 * total[0, 0]
    gscale[0] = total[1, 0]
    for copy in sends:
        copy.wait_send()


def body(peers, images, texts, log_scale):
    _, rows, width = images.shape
    grad = jax.ShapeDtypeStruct(images.shape, jnp.bfloat16)
    scalar = jax.ShapeDtypeStruct((1,), jnp.float32)
    dma = pltpu.SemaphoreType.DMA
    vmem = pltpu.VMEM
    gimg, gtxt, loss, gscale = pl.pallas_call(
        functools.partial(kernel, peers),
        out_shape=(grad, grad, scalar, scalar),
        in_specs=[pl.BlockSpec(memory_space=pltpu.SMEM)] + [pl.BlockSpec(memory_space=pltpu.HBM)] * 2,
        out_specs=(pl.BlockSpec(memory_space=vmem),) * 2 + (pl.BlockSpec(memory_space=pltpu.SMEM),) * 2,
        scratch_shapes=[
            vmem((2, KEYS * rows, width), jnp.bfloat16),
            vmem((2, rows, KEYS * rows), jnp.float32),
            vmem((2, rows, KEYS * rows), jnp.float32),
            vmem((2, rows, KEYS * rows), jnp.bfloat16),
            vmem((2, rows, 1), jnp.float32),
            vmem((2, rows, 1), jnp.float32),
            vmem((2, rows, 1), jnp.float32),
            vmem((2, 8, rows), jnp.float32),
            vmem((2, 8, KEYS * rows), jnp.float32),
            vmem((3, 8, 8, 128), jnp.float32),
            dma((2,)),
            dma((4, 2, PARTS)),
            dma((2, KEYS, PARTS)),
            dma((2, KEYS)),
            dma((2, KEYS)),
            dma((3, 8)),
            dma((3,)),
        ],
        compiler_params=pltpu.CompilerParams(
            collective_id=0, has_side_effects=True, vmem_limit_bytes=56 * 2**20),
        cost_estimate=pl.CostEstimate(flops=20 * 2 * rows * rows * width, bytes_accessed=4 * rows * width * 2, transcendentals=30 * rows * rows),
        name="band_clip",
    )(log_scale.reshape(1), images, texts)
    return gimg, gtxt, loss.reshape(()), gscale.reshape(())


def solution(mesh):
    placed = (P("rep", "blk", None), P("rep", "blk", None), P())
    return jax.shard_map(
        functools.partial(body, mesh.shape["blk"]),
        mesh=mesh,
        in_specs=placed,
        out_specs=(P("rep", "blk", None), P("rep", "blk", None), P(), P()),
        check_vma=False,
    )
```

```python
import functools
import math

import jax
import jax.numpy as jnp
from jax import lax
from jax.experimental import pallas as pl
from jax.experimental.pallas import tpu as pltpu
from jax.sharding import PartitionSpec as P

HOPS = 4
KEYS = HOPS + 1
LOG2E = math.log2(math.e)
LN2 = math.log(2.0)
MESH = pl.DeviceIdType.MESH
PARTS = 3
HOP_PARTS = 6
LINE = 16
TILE = 128


def kernel(peers, ls_hbm, img, txt, acc0, acc1, sums, ls, acc, X, S, A, lanes, stats, near_part, far_part, LR, AR,
           lsem, ssem, rsem, hop_ssem, hop_rsem, near_ssem, near_rsem, far_ssem, far_rsem, ar_ssem, ar_rsem, known):
    rows, width = img.shape[1], img.shape[2]
    piece = rows // PARTS
    b = lax.axis_index("blk")
    rep = lax.axis_index("rep")
    core = lax.rem(b, 2)
    other = 1 - core
    sib = b + 1 - 2 * core

    def ring(d):
        return (lax.rem(b + d + peers, peers), rep)

    step = (ring(2), ring(-2))
    sibling = (sib, rep)
    own = (txt, img)

    def remote(src, dst, s, r, d):
        return pltpu.make_async_remote_copy(
            src_ref=src, dst_ref=dst, send_sem=s, recv_sem=r, device_id=d, device_id_type=MESH)

    def signal(sem, d):
        pl.semaphore_signal(sem, inc=1, device_id=d, device_id_type=MESH)

    barrier = pltpu.get_barrier_semaphore()
    greeted = (step[0], step[1], sibling, (b, 1 - rep))
    for d in greeted:
        signal(barrier, d)
    loads = [pltpu.make_async_copy(own[p].at[0], X.at[p, pl.ds(0, rows)], lsem.at[p]) for p in range(2)]
    loads.append(pltpu.make_async_copy(ls_hbm, ls, lsem.at[2]))
    for load in loads:
        load.start()
    pl.semaphore_wait(barrier, len(greeted))

    def at(k, j):
        return pl.ds(pl.multiple_of(rows * k + j * piece, piece), piece)

    def arrived(p, k, j):
        here = X.at[p, at(k, j)]
        remote(here, here, ssem.at[0, 0], rsem.at[p, k, j], sibling).wait_recv()

    hop_piece = rows // HOP_PARTS

    def hop_at(k, i):
        return pl.ds(pl.multiple_of(rows * k + i * hop_piece, hop_piece), hop_piece)

    def hopped(p, far, i):
        here = X.at[p, hop_at(2 + 2 * far, i)]
        remote(here, here, hop_ssem.at[0, 0, 0], hop_rsem.at[p, far, i], sibling).wait_recv()

    def forward(i):
        for p in range(2):
            remote(X.at[p, hop_at(2, i)], X.at[p, hop_at(4, i)], hop_ssem.at[p, 1, i], hop_rsem.at[p, 1, i], step[p]).start()

    for i in range(HOP_PARTS):
        for p in range(2):
            remote(own[p].at[0, pl.ds(i * hop_piece, hop_piece)], X.at[p, hop_at(2, i)], hop_ssem.at[p, 0, i], hop_rsem.at[p, 0, i], step[p]).start()
    for load in loads:
        load.wait()
    for j in range(PARTS):
        remote(X.at[core, at(0, j)], X.at[core, at(1, j)], ssem.at[0, j], rsem.at[core, 1, j], sibling).start()

    scale2 = jnp.exp(ls[...]) * LOG2E
    lanes[0] = jnp.full(lanes.shape[1:], -jnp.inf, jnp.float32)
    lanes[1:3] = jnp.zeros((2,) + lanes.shape[1:], jnp.float32)
    acc[...] = jnp.zeros(acc.shape, jnp.float32)

    def logits(qp, qk, kp, first, n):
        return scale2 * lax.dot_general(
            X[qp, pl.ds(pl.multiple_of(qk * rows, TILE), rows)], X[kp, pl.ds(pl.multiple_of(first, TILE), n)],
            (((1,), (1,)), ((), ())), preferred_element_type=jnp.float32)

    def count(a, s):
        parts = [s[:, i:i + TILE] for i in range(0, s.shape[1], TILE)]
        old = lanes[0, a]
        top = functools.reduce(jnp.maximum, parts, old)
        fade = jnp.exp2(old - top)
        total, weighted = fade * lanes[1, a], fade * lanes[2, a]
        for part in parts:
            e = jnp.exp2(part - top)
            total = total + e
            weighted = weighted + e * part
        lanes[0, a], lanes[1, a], lanes[2, a] = top, total, weighted

    def score(p, first, n):
        s = logits(1 - p, 0, p, first, n)
        for i in range(n // TILE):
            S[p, first // TILE + i] = s[:, i * TILE:(i + 1) * TILE]
        count(p, s)

    @pl.loop(0, 2)
    def _(p):
        score(p, 0, rows)

    for j in range(PARTS):
        arrived(other, 1, j)
    score(other, rows, rows)

    def spread(r):
        for d in (4 << r, -(4 << r)):
            signal(known.at[r], ring(d))

    def learn(r):
        pl.semaphore_wait(known.at[r], 2)

    def near_scores(j):
        @pl.loop(0, 2)
        def _(p):
            score(p, 2 * rows + j * piece, piece)

        @pl.loop(0, 2)
        def _(i):
            p = lax.rem(core + i, 2)
            k = 1 + 2 * i

            @pl.when(jnp.logical_or(i == 1, j < PARTS - 1))
            def _():
                arrived(p, k, j)

            score(p, k * rows + j * piece, piece)

    @pl.loop(0, PARTS)
    def _(j):
        per = HOP_PARTS // PARTS
        for p in range(2):
            hopped(p, 0, j * per)

        @pl.when(j == 0)
        def _():
            spread(0)

        for i in range(1, per):
            for p in range(2):
                hopped(p, 0, j * per + i)
        for p in range(2):
            k = 3 - 2 * core if p == 0 else 1 + 2 * core
            remote(X.at[p, at(2, j)], X.at[p, at(k, j)], ssem.at[1 + p, j], rsem.at[p, k, j], sibling).start()

        @pl.when(j == 0)
        def _():
            forward(0)
            learn(0)
            spread(1)

        @pl.when(j == 1)
        def _():
            forward(1)
            learn(1)
            spread(2)

        @pl.when(j < PARTS - 1)
        def _():
            near_scores(j)

    count(3, logits(core, 2, other, 2 * rows, rows))
    arrived(core, 1, PARTS - 1)

    @pl.loop(0, 2)
    def _(i):
        count(2, logits(other, 2, core, (1 + i) * rows, rows))

    def lay(a):
        top = jnp.max(lanes[0, a].T, axis=0, keepdims=True)
        fade = jnp.exp2(lanes[0, a].T - top)
        total = jnp.sum(fade * lanes[1, a].T, axis=0, keepdims=True)
        weighted = jnp.sum(fade * lanes[2, a].T, axis=0, keepdims=True)
        for j in range(PARTS):
            cols = slice(j * piece, (j + 1) * piece)
            stats[a, 0, j:j + 1] = top[:, cols]
            stats[a, 0, PARTS + j:PARTS + j + 1] = total[:, cols]
            stats[a, 1, j:j + 1] = weighted[:, cols]

    for i in range(2):
        lay(3 - i)
    for q in range(2):
        a = 3 - core if q == 0 else 2 + core
        far_part[q, 2] = stats[a]
        for k in (0, 1, 3, 4):
            there = ring(k - 2 if q == 0 else 2 - k)
            part = pl.ds(0, 2 if k == 0 else 1)
            remote(stats.at[a, part], far_part.at[q, k, part], far_ssem.at[q, k], far_rsem.at[q, k], there).start()
    near_scores(PARTS - 1)
    for p in range(2):
        lay(p)
        near_part[1 - p, 0] = stats[p]
    for q in range(2):
        for k in range(1, KEYS):
            part = pl.ds(0, 1)
            remote(stats.at[1 - q, part], near_part.at[q, k, part], near_ssem.at[q, k], near_rsem.at[q, k], ring(k if q == 0 else -k)).start()
    forward(2)
    learn(2)
    spread(3)
    diag = jnp.zeros((), jnp.float32)
    one = (lax.broadcasted_iota(jnp.int32, (piece, piece), 0) == lax.broadcasted_iota(jnp.int32, (piece, piece), 1)).astype(jnp.float32)
    for j in range(PARTS):
        diag = diag + jnp.sum(S[0, j, pl.ds(j * piece, piece), :] * one)

    def merge(q, k):
        m1, m2 = near_part[q, k, 0, 0:PARTS], far_part[q, k, 0, 0:PARTS]
        l1, l2 = near_part[q, k, 0, PARTS:2 * PARTS], far_part[q, k, 0, PARTS:2 * PARTS]
        top = jnp.maximum(m1, m2)
        f1, f2 = jnp.exp2(m1 - top), jnp.exp2(m2 - top)
        total = f1 * l1 + f2 * l2
        half = top + jnp.log2(total) + 1.0
        for j in range(PARTS):
            LR[q, k, j, 0:1] = half[j:j + 1]
        return half, f1, f2, total

    def part_here(here, s, r):
        remote(here, here, s, r, sibling).wait_recv()

    lse_sum = -2.0 * rows
    pull = 0.0
    for q in range(2):
        part_here(far_part.at[q, 0], far_ssem.at[q, 0], far_rsem.at[q, 0])
        half, f1, f2, total = merge(q, 0)
        lse_sum = lse_sum + jnp.sum(half)
        pull = pull + jnp.sum((f1 * near_part[q, 0, 1, 0:PARTS] + f2 * far_part[q, 0, 1, 0:PARTS]) / total)
        for j in range(PARTS):
            A[1 - q, pl.ds(j * piece, piece)] = jnp.broadcast_to(half[j:j + 1], (TILE, piece)).T

    z, xl, y = lax.rem(b // 2, LINE), lax.rem(b // (2 * LINE), 2), b // (4 * LINE)
    x = 2 * rep + xl
    sizes = (LINE, LINE, 2)
    place = (z, 4 * y + x, core)

    def far_first(n):
        return sorted(range(n), key=lambda d: -min(d, n - d))

    def others(stage):
        if stage == 0:
            return [(b + 2 * (lax.rem(z + d, LINE) - z), rep) for d in far_first(LINE) if d]
        if stage == 1:
            found = []
            for dy, dx in sorted(((i, j) for i in range(4) for j in range(4)), key=lambda d: -sum(min(i, 4 - i) for i in d)):
                if dy or dx:
                    ny, nx = lax.rem(y + dy, 4), lax.rem(x + dx, 4)
                    found.append((4 * LINE * ny + 2 * LINE * lax.rem(nx, 2) + lax.rem(b, 2 * LINE), nx // 2))
            return found
        return [sibling]

    def share(stage, value):
        mine = AR.at[stage, place[stage]]
        mine[...] = value
        for d in others(stage):
            remote(mine, mine, ar_ssem.at[stage], ar_rsem.at[stage], d).start()

    def gather(stage):
        rest = AR.at[stage, pl.ds(0, sizes[stage] - 1)]
        remote(rest, rest, ar_ssem.at[stage], ar_rsem.at[stage], sibling).wait_recv()
        value = AR[stage, 0]
        for i in range(1, sizes[stage]):
            value = value + AR[stage, i]
        return value

    top_row = lax.broadcasted_iota(jnp.int32, (8, TILE), 0) == 0
    share(0, jnp.where(top_row, lse_sum - 2.0 * diag, 0.5 * pull - diag))
    for i in range(3, HOP_PARTS):
        forward(i)
    learn(3)
    spread(4)

    def halves(p, k, j, s):
        return jnp.exp2(s - A[p]) + jnp.exp2(s - LR[p, k, j, 0:1])

    for q in range(2):
        for k in range(1, KEYS):
            part = pl.ds(0, 1)
            part_here(near_part.at[q, k, part], near_ssem.at[q, k], near_rsem.at[q, k])
            if k != 2:
                part_here(far_part.at[q, k, part], far_ssem.at[q, k], far_rsem.at[q, k])
            merge(q, k)
    learn(4)
    spread(5)

    row_id = lax.broadcasted_iota(jnp.int32, (rows, piece), 0)
    col_id = lax.broadcasted_iota(jnp.int32, (rows, piece), 1)

    def near(p, k):
        hit = jnp.where(k == 0, 1.0, 0.0)
        g = [halves(p, k, j, S[p, k * PARTS + j]) - jnp.where(row_id == col_id + j * piece, hit, 0.0) for j in range(PARTS)]
        g = jnp.concatenate([t.astype(jnp.bfloat16) for t in g], axis=1)
        acc[p] += jnp.dot(g, X[p, pl.ds(pl.multiple_of(k * rows, TILE), rows)], preferred_element_type=jnp.float32)

    @pl.loop(0, 3)
    def _(k):
        near(0, k)
        near(1, k)

    near(other, 3)

    def far(p, slots, j):
        x = [X[p, at(k, j)] for k in slots]
        x = x[0] if len(x) == 1 else jnp.concatenate(x, axis=0)
        s = scale2 * lax.dot_general(X[1 - p, pl.ds(0, rows)], x, (((1,), (1,)), ((), ())), preferred_element_type=jnp.float32)
        g = [halves(p, k, j, s[:, i * piece:(i + 1) * piece]).astype(jnp.bfloat16) for i, k in enumerate(slots)]
        g = g[0] if len(g) == 1 else jnp.concatenate(g, axis=1)
        acc[p] += jnp.dot(g, x, preferred_element_type=jnp.float32)

    def far_pieces(j):
        per = HOP_PARTS // PARTS
        for i in range(per):
            hopped(other, 1, j * per + i)
        remote(X.at[other, at(4, j)], X.at[other, at(3, j)], ssem.at[3, j], rsem.at[other, 3, j], sibling).start()
        far(other, (4,), j)
        for i in range(per):
            hopped(core, 1, j * per + i)
        arrived(core, 3, j)
        far(core, (3, 4), j)

    @pl.loop(0, PARTS - 1)
    def _(j):
        far_pieces(j)

    learn(5)
    share(1, gather(0))
    far_pieces(PARTS - 1)
    share(2, gather(1))
    scale = jnp.exp(ls[...])
    acc0[0] = scale * acc[0]
    acc1[0] = scale * acc[1]
    unit = LN2 / (2 * peers * rows)
    sums[...] = gather(2) * jnp.where(top_row, 0.5 * unit, unit)

    for j in range(PARTS):
        for kind in range(4):
            here = X.at[0, at(0, 0)]
            remote(here, here, ssem.at[kind, j], rsem.at[0, 0, 0], sibling).wait_send()
    for i in range(HOP_PARTS):
        for p in range(2):
            for far_hop in range(2):
                here = X.at[0, hop_at(0, 0)]
                remote(here, here, hop_ssem.at[p, far_hop, i], hop_rsem.at[0, 0, 0], sibling).wait_send()
    for q in range(2):
        for k in range(KEYS):
            here = stats.at[0, pl.ds(0, 2 if k == 0 else 1)]
            if k != 2:
                remote(here, here, far_ssem.at[q, k], far_rsem.at[q, k], sibling).wait_send()
            if k != 0:
                remote(here, here, near_ssem.at[q, k], near_rsem.at[q, k], sibling).wait_send()
    for stage in range(3):
        rest = AR.at[stage, pl.ds(0, sizes[stage] - 1)]
        remote(rest, rest, ar_ssem.at[stage], ar_rsem.at[stage], sibling).wait_send()


def body(peers, images, texts, log_scale):
    _, rows, width = images.shape
    f32 = jnp.float32
    dma = pltpu.SemaphoreType.DMA
    vmem = pltpu.VMEM
    side = jax.ShapeDtypeStruct((1, rows, width), f32)
    acc0, acc1, sums = pl.pallas_call(
        functools.partial(kernel, peers),
        out_shape=(side, side, jax.ShapeDtypeStruct((8, TILE), f32)),
        in_specs=[pl.BlockSpec(memory_space=pl.ANY)] + [pl.BlockSpec(memory_space=pltpu.HBM)] * 2,
        out_specs=(pl.BlockSpec(memory_space=vmem),) * 3,
        scratch_shapes=[
            vmem((1, 1), f32),
            vmem((2, rows, width), f32),
            vmem((2, KEYS * rows, width), jnp.bfloat16),
            vmem((2, HOPS * PARTS, rows, rows // PARTS), f32),
            vmem((2, rows, TILE), f32),
            vmem((3, 4, rows, TILE), f32),
            vmem((4, 2, 8, TILE), f32),
            vmem((2, KEYS, 2, 8, TILE), f32),
            vmem((2, KEYS, 2, 8, TILE), f32),
            vmem((2, KEYS, PARTS, 8, TILE), f32),
            vmem((3, LINE, 8, TILE), f32),
            dma((3,)),
            dma((4, PARTS)),
            dma((2, KEYS, PARTS)),
            dma((2, 2, HOP_PARTS)),
            dma((2, 2, HOP_PARTS)),
            dma((2, KEYS)),
            dma((2, KEYS)),
            dma((2, KEYS)),
            dma((2, KEYS)),
            dma((3,)),
            dma((3,)),
            pltpu.SemaphoreType.REGULAR((6,)),
        ],
        compiler_params=pltpu.CompilerParams(
            collective_id=0, has_side_effects=True, vmem_limit_bytes=40 * 2**20),
        cost_estimate=pl.CostEstimate(
            flops=23 * 2 * rows * rows * width, bytes_accessed=4 * rows * width * 2, transcendentals=30 * rows * rows),
        name="band_clip",
    )(log_scale.reshape(1, 1), *(pltpu.with_memory_space_constraint(x, pltpu.HBM) for x in (images, texts)))
    return acc0.astype(jnp.bfloat16), acc1.astype(jnp.bfloat16), sums[0, 0], sums[1, 0]


def solution(mesh):
    placed = (P("rep", "blk", None), P("rep", "blk", None), P())
    return jax.shard_map(
        functools.partial(body, mesh.shape["blk"]),
        mesh=mesh,
        in_specs=placed,
        out_specs=(P("rep", "blk", None), P("rep", "blk", None), P(), P()),
        check_vma=False,
    )
```

```python
import functools
import math

import jax
import jax.numpy as jnp
from jax import lax
from jax.experimental import pallas as pl
from jax.experimental.pallas import tpu as pltpu
from jax.sharding import PartitionSpec as P

HOPS = 4
KEYS = HOPS + 1
LOG2E = math.log2(math.e)
LN2 = math.log(2.0)
MESH = pl.DeviceIdType.MESH
PARTS = 3
HOP_PARTS = 6
LINE = 16
TILE = 128


def kernel(peers, ls_hbm, img, txt, gimg, gtxt, sums, ls, acc, X, S, A, lanes, stats, near_part, far_part, LR, AR,
           lsem, ssem, rsem, hop_ssem, hop_rsem, near_ssem, near_rsem, far_ssem, far_rsem, ar_ssem, ar_rsem, known):
    rows, width = img.shape[1], img.shape[2]
    piece = rows // PARTS
    b = lax.axis_index("blk")
    rep = lax.axis_index("rep")
    core = lax.rem(b, 2)
    other = 1 - core
    sib = b + 1 - 2 * core

    def ring(d):
        return (lax.rem(b + d + peers, peers), rep)

    step = (ring(2), ring(-2))
    sibling = (sib, rep)
    own = (txt, img)

    def remote(src, dst, s, r, d):
        return pltpu.make_async_remote_copy(
            src_ref=src, dst_ref=dst, send_sem=s, recv_sem=r, device_id=d, device_id_type=MESH)

    def signal(sem, d):
        pl.semaphore_signal(sem, inc=1, device_id=d, device_id_type=MESH)

    barrier = pltpu.get_barrier_semaphore()
    greeted = (step[0], step[1], sibling, (b, 1 - rep))
    for d in greeted:
        signal(barrier, d)
    loads = [pltpu.make_async_copy(own[p].at[0], X.at[p, pl.ds(0, rows)], lsem.at[p]) for p in range(2)]
    loads.append(pltpu.make_async_copy(ls_hbm, ls, lsem.at[2]))
    for load in loads:
        load.start()
    pl.semaphore_wait(barrier, len(greeted))

    def at(k, j):
        return pl.ds(pl.multiple_of(rows * k + j * piece, piece), piece)

    def arrived(p, k, j):
        here = X.at[p, at(k, j)]
        remote(here, here, ssem.at[0, 0], rsem.at[p, k, j], sibling).wait_recv()

    hop_piece = rows // HOP_PARTS

    def hop_at(k, i):
        return pl.ds(pl.multiple_of(rows * k + i * hop_piece, hop_piece), hop_piece)

    def hopped(p, far, i):
        here = X.at[p, hop_at(2 + 2 * far, i)]
        remote(here, here, hop_ssem.at[0, 0, 0], hop_rsem.at[p, far, i], sibling).wait_recv()

    def forward(i):
        for p in range(2):
            remote(X.at[p, hop_at(2, i)], X.at[p, hop_at(4, i)], hop_ssem.at[p, 1, i], hop_rsem.at[p, 1, i], step[p]).start()

    for i in range(HOP_PARTS):
        for p in range(2):
            remote(own[p].at[0, pl.ds(i * hop_piece, hop_piece)], X.at[p, hop_at(2, i)], hop_ssem.at[p, 0, i], hop_rsem.at[p, 0, i], step[p]).start()
    for load in loads:
        load.wait()
    for j in range(PARTS):
        remote(X.at[core, at(0, j)], X.at[core, at(1, j)], ssem.at[0, j], rsem.at[core, 1, j], sibling).start()

    scale2 = jnp.exp(ls[...]) * LOG2E
    lanes[0] = jnp.full(lanes.shape[1:], -jnp.inf, jnp.float32)
    lanes[1:3] = jnp.zeros((2,) + lanes.shape[1:], jnp.float32)
    acc[...] = jnp.zeros(acc.shape, jnp.float32)

    def logits(qp, qk, kp, first, n):
        return scale2 * lax.dot_general(
            X[qp, pl.ds(pl.multiple_of(qk * rows, TILE), rows)], X[kp, pl.ds(pl.multiple_of(first, TILE), n)],
            (((1,), (1,)), ((), ())), preferred_element_type=jnp.float32)

    def count(a, s):
        parts = [s[:, i:i + TILE] for i in range(0, s.shape[1], TILE)]
        old = lanes[0, a]
        top = functools.reduce(jnp.maximum, parts, old)
        fade = jnp.exp2(old - top)
        total, weighted = fade * lanes[1, a], fade * lanes[2, a]
        for part in parts:
            e = jnp.exp2(part - top)
            total = total + e
            weighted = weighted + e * part
        lanes[0, a], lanes[1, a], lanes[2, a] = top, total, weighted

    def score(p, first, n):
        s = logits(1 - p, 0, p, first, n)
        for i in range(n // TILE):
            S[p, first // TILE + i] = s[:, i * TILE:(i + 1) * TILE]
        count(p, s)

    @pl.loop(0, 2)
    def _(p):
        score(p, 0, rows)

    for j in range(PARTS):
        arrived(other, 1, j)
    score(other, rows, rows)

    def spread(r):
        for d in (4 << r, -(4 << r)):
            signal(known.at[r], ring(d))

    def learn(r):
        pl.semaphore_wait(known.at[r], 2)

    def near_scores(j):
        @pl.loop(0, 2)
        def _(p):
            score(p, 2 * rows + j * piece, piece)

        @pl.loop(0, 2)
        def _(i):
            p = lax.rem(core + i, 2)
            k = 1 + 2 * i

            @pl.when(jnp.logical_or(i == 1, j < PARTS - 1))
            def _():
                arrived(p, k, j)

            score(p, k * rows + j * piece, piece)

    @pl.loop(0, PARTS)
    def _(j):
        per = HOP_PARTS // PARTS
        for p in range(2):
            hopped(p, 0, j * per)

        @pl.when(j == 0)
        def _():
            spread(0)

        for i in range(1, per):
            for p in range(2):
                hopped(p, 0, j * per + i)
        for p in range(2):
            k = 3 - 2 * core if p == 0 else 1 + 2 * core
            remote(X.at[p, at(2, j)], X.at[p, at(k, j)], ssem.at[1 + p, j], rsem.at[p, k, j], sibling).start()

        @pl.when(j == 0)
        def _():
            forward(0)
            learn(0)
            spread(1)

        @pl.when(j == 1)
        def _():
            for i in (1, 2):
                forward(i)
            learn(1)
            spread(2)

        @pl.when(j < PARTS - 1)
        def _():
            near_scores(j)

    count(3, logits(core, 2, other, 2 * rows, rows))
    arrived(core, 1, PARTS - 1)

    @pl.loop(0, 2)
    def _(i):
        count(2, logits(other, 2, core, (1 + i) * rows, rows))

    def lay(a):
        top = jnp.max(lanes[0, a].T, axis=0, keepdims=True)
        fade = jnp.exp2(lanes[0, a].T - top)
        total = jnp.sum(fade * lanes[1, a].T, axis=0, keepdims=True)
        weighted = jnp.sum(fade * lanes[2, a].T, axis=0, keepdims=True)
        for j in range(PARTS):
            cols = slice(j * piece, (j + 1) * piece)
            stats[a, 0, j:j + 1] = top[:, cols]
            stats[a, 0, PARTS + j:PARTS + j + 1] = total[:, cols]
            stats[a, 1, j:j + 1] = weighted[:, cols]

    for i in range(2):
        lay(3 - i)
    for q in range(2):
        a = 3 - core if q == 0 else 2 + core
        far_part[q, 2] = stats[a]
        for k in (0, 1, 3, 4):
            there = ring(k - 2 if q == 0 else 2 - k)
            part = pl.ds(0, 2 if k == 0 else 1)
            remote(stats.at[a, part], far_part.at[q, k, part], far_ssem.at[q, k], far_rsem.at[q, k], there).start()
    near_scores(PARTS - 1)
    for p in range(2):
        lay(p)
        near_part[1 - p, 0] = stats[p]
    for q in range(2):
        for k in range(1, KEYS):
            part = pl.ds(0, 1)
            remote(stats.at[1 - q, part], near_part.at[q, k, part], near_ssem.at[q, k], near_rsem.at[q, k], ring(k if q == 0 else -k)).start()
    forward(3)
    learn(2)
    spread(3)
    diag = jnp.zeros((), jnp.float32)
    one = (lax.broadcasted_iota(jnp.int32, (piece, piece), 0) == lax.broadcasted_iota(jnp.int32, (piece, piece), 1)).astype(jnp.float32)
    for j in range(PARTS):
        diag = diag + jnp.sum(S[0, j, pl.ds(j * piece, piece), :] * one)

    def merge(q, k):
        m1, m2 = near_part[q, k, 0, 0:PARTS], far_part[q, k, 0, 0:PARTS]
        l1, l2 = near_part[q, k, 0, PARTS:2 * PARTS], far_part[q, k, 0, PARTS:2 * PARTS]
        top = jnp.maximum(m1, m2)
        f1, f2 = jnp.exp2(m1 - top), jnp.exp2(m2 - top)
        total = f1 * l1 + f2 * l2
        half = top + jnp.log2(total) + 1.0
        for j in range(PARTS):
            LR[q, k, j, 0:1] = half[j:j + 1]
        return half, f1, f2, total

    def part_here(here, s, r):
        remote(here, here, s, r, sibling).wait_recv()

    lse_sum = -2.0 * rows
    pull = 0.0
    for q in range(2):
        part_here(far_part.at[q, 0], far_ssem.at[q, 0], far_rsem.at[q, 0])
        half, f1, f2, total = merge(q, 0)
        lse_sum = lse_sum + jnp.sum(half)
        pull = pull + jnp.sum((f1 * near_part[q, 0, 1, 0:PARTS] + f2 * far_part[q, 0, 1, 0:PARTS]) / total)
        for j in range(PARTS):
            A[1 - q, pl.ds(j * piece, piece)] = jnp.broadcast_to(half[j:j + 1], (TILE, piece)).T

    z, xl, y = lax.rem(b // 2, LINE), lax.rem(b // (2 * LINE), 2), b // (4 * LINE)
    x = 2 * rep + xl
    sizes = (LINE, LINE, 2)
    place = (z, 4 * y + x, core)

    def far_first(n):
        return sorted(range(n), key=lambda d: -min(d, n - d))

    def others(stage):
        if stage == 0:
            return [(b + 2 * (lax.rem(z + d, LINE) - z), rep) for d in far_first(LINE) if d]
        if stage == 1:
            found = []
            for dy, dx in sorted(((i, j) for i in range(4) for j in range(4)), key=lambda d: -sum(min(i, 4 - i) for i in d)):
                if dy or dx:
                    ny, nx = lax.rem(y + dy, 4), lax.rem(x + dx, 4)
                    found.append((4 * LINE * ny + 2 * LINE * lax.rem(nx, 2) + lax.rem(b, 2 * LINE), nx // 2))
            return found
        return [sibling]

    def share(stage, value):
        mine = AR.at[stage, place[stage]]
        mine[...] = value
        for d in others(stage):
            remote(mine, mine, ar_ssem.at[stage], ar_rsem.at[stage], d).start()

    def gather(stage):
        rest = AR.at[stage, pl.ds(0, sizes[stage] - 1)]
        remote(rest, rest, ar_ssem.at[stage], ar_rsem.at[stage], sibling).wait_recv()
        value = AR[stage, 0]
        for i in range(1, sizes[stage]):
            value = value + AR[stage, i]
        return value

    top_row = lax.broadcasted_iota(jnp.int32, (8, TILE), 0) == 0
    share(0, jnp.where(top_row, lse_sum - 2.0 * diag, 0.5 * pull - diag))
    for i in (4, 5):
        forward(i)
    learn(3)
    spread(4)
    def halves(p, k, j, s):
        return jnp.exp2(s - A[p]) + jnp.exp2(s - LR[p, k, j, 0:1])

    for q in range(2):
        for k in range(1, KEYS):
            part = pl.ds(0, 1)
            part_here(near_part.at[q, k, part], near_ssem.at[q, k], near_rsem.at[q, k])
            if k != 2:
                part_here(far_part.at[q, k, part], far_ssem.at[q, k], far_rsem.at[q, k])
            merge(q, k)
    learn(4)
    spread(5)

    row_id = lax.broadcasted_iota(jnp.int32, (rows, piece), 0)
    col_id = lax.broadcasted_iota(jnp.int32, (rows, piece), 1)

    def near(p, k):
        hit = jnp.where(k == 0, 1.0, 0.0)
        g = [halves(p, k, j, S[p, k * PARTS + j]) - jnp.where(row_id == col_id + j * piece, hit, 0.0) for j in range(PARTS)]
        g = jnp.concatenate([t.astype(jnp.bfloat16) for t in g], axis=1)
        acc[p] += jnp.dot(g, X[p, pl.ds(pl.multiple_of(k * rows, TILE), rows)], preferred_element_type=jnp.float32)

    @pl.loop(0, 3)
    def _(k):
        near(0, k)
        near(1, k)

    near(other, 3)

    def far(j, *sides):
        keys, grads = [], []
        for p, slots in sides:
            x = [X[p, at(k, j)] for k in slots]
            keys.append(x[0] if len(x) == 1 else jnp.concatenate(x, axis=0))
        scores = [scale2 * lax.dot_general(X[1 - p, pl.ds(0, rows)], x, (((1,), (1,)), ((), ())), preferred_element_type=jnp.float32)
                  for (p, _), x in zip(sides, keys)]
        for (p, slots), s in zip(sides, scores):
            g = [halves(p, k, j, s[:, i * piece:(i + 1) * piece]).astype(jnp.bfloat16) for i, k in enumerate(slots)]
            grads.append(g[0] if len(g) == 1 else jnp.concatenate(g, axis=1))
        for (p, _), g, x in zip(sides, grads, keys):
            acc[p] += jnp.dot(g, x, preferred_element_type=jnp.float32)

    def far_here(p, j):
        per = HOP_PARTS // PARTS
        for i in range(per):
            hopped(p, 1, j * per + i)

    def far_relay(j):
        far_here(other, j)
        remote(X.at[other, at(4, j)], X.at[other, at(3, j)], ssem.at[3, j], rsem.at[other, 3, j], sibling).start()

    for j in range(PARTS - 1):
        far_relay(j)
        far_here(core, j)
        arrived(core, 3, j)
        far(j, (other, (4,)), (core, (3, 4)))
    learn(5)
    share(1, gather(0))
    far_relay(PARTS - 1)
    far(PARTS - 1, (other, (4,)))
    far_here(core, PARTS - 1)
    arrived(core, 3, PARTS - 1)
    far(PARTS - 1, (core, (3, 4)))
    share(2, gather(1))
    scale = jnp.exp(ls[...])
    gimg[0] = (scale * acc[0]).astype(jnp.bfloat16)
    gtxt[0] = (scale * acc[1]).astype(jnp.bfloat16)
    unit = LN2 / (2 * peers * rows)
    sums[...] = gather(2) * jnp.where(top_row, 0.5 * unit, unit)

    for j in range(PARTS):
        for kind in range(4):
            here = X.at[0, at(0, 0)]
            remote(here, here, ssem.at[kind, j], rsem.at[0, 0, 0], sibling).wait_send()
    for i in range(HOP_PARTS):
        for p in range(2):
            for far_hop in range(2):
                here = X.at[0, hop_at(0, 0)]
                remote(here, here, hop_ssem.at[p, far_hop, i], hop_rsem.at[0, 0, 0], sibling).wait_send()
    for q in range(2):
        for k in range(KEYS):
            here = stats.at[0, pl.ds(0, 2 if k == 0 else 1)]
            if k != 2:
                remote(here, here, far_ssem.at[q, k], far_rsem.at[q, k], sibling).wait_send()
            if k != 0:
                remote(here, here, near_ssem.at[q, k], near_rsem.at[q, k], sibling).wait_send()
    for stage in range(3):
        rest = AR.at[stage, pl.ds(0, sizes[stage] - 1)]
        remote(rest, rest, ar_ssem.at[stage], ar_rsem.at[stage], sibling).wait_send()


def body(peers, images, texts, log_scale):
    _, rows, width = images.shape
    f32 = jnp.float32
    dma = pltpu.SemaphoreType.DMA
    vmem = pltpu.VMEM
    side = jax.ShapeDtypeStruct((1, rows, width), jnp.bfloat16)
    gimg, gtxt, sums = pl.pallas_call(
        functools.partial(kernel, peers),
        out_shape=(side, side, jax.ShapeDtypeStruct((8, TILE), f32)),
        in_specs=[pl.BlockSpec(memory_space=pl.ANY)] + [pl.BlockSpec(memory_space=pltpu.HBM)] * 2,
        out_specs=(pl.BlockSpec(memory_space=vmem),) * 3,
        scratch_shapes=[
            vmem((1, 1), f32),
            vmem((2, rows, width), f32),
            vmem((2, KEYS * rows, width), jnp.bfloat16),
            vmem((2, HOPS * PARTS, rows, rows // PARTS), f32),
            vmem((2, rows, TILE), f32),
            vmem((3, 4, rows, TILE), f32),
            vmem((4, 2, 8, TILE), f32),
            vmem((2, KEYS, 2, 8, TILE), f32),
            vmem((2, KEYS, 2, 8, TILE), f32),
            vmem((2, KEYS, PARTS, 8, TILE), f32),
            vmem((3, LINE, 8, TILE), f32),
            dma((3,)),
            dma((4, PARTS)),
            dma((2, KEYS, PARTS)),
            dma((2, 2, HOP_PARTS)),
            dma((2, 2, HOP_PARTS)),
            dma((2, KEYS)),
            dma((2, KEYS)),
            dma((2, KEYS)),
            dma((2, KEYS)),
            dma((3,)),
            dma((3,)),
            pltpu.SemaphoreType.REGULAR((6,)),
        ],
        compiler_params=pltpu.CompilerParams(
            collective_id=0, has_side_effects=True, vmem_limit_bytes=40 * 2**20),
        cost_estimate=pl.CostEstimate(
            flops=23 * 2 * rows * rows * width, bytes_accessed=4 * rows * width * 2, transcendentals=30 * rows * rows),
        name="band_clip",
    )(log_scale.reshape(1, 1), *(pltpu.with_memory_space_constraint(x, pltpu.HBM) for x in (images, texts)))
    return gimg, gtxt, sums[0, 0], sums[1, 0]


def solution(mesh):
    placed = (P("rep", "blk", None), P("rep", "blk", None), P())
    return jax.shard_map(
        functools.partial(body, mesh.shape["blk"]),
        mesh=mesh,
        in_specs=placed,
        out_specs=(P("rep", "blk", None), P("rep", "blk", None), P(), P()),
        check_vma=False,
    )
```

```python
import functools
import math

import jax
import jax.numpy as jnp
from jax import lax
from jax.experimental import pallas as pl
from jax.experimental.pallas import tpu as pltpu
from jax.sharding import PartitionSpec as P

HOPS = 4
KEYS = HOPS + 1
LOG2E = math.log2(math.e)
LN2 = math.log(2.0)
MESH = pl.DeviceIdType.MESH
PARTS = 3
HOP_PARTS = 6
LINE = 16
TILE = 128


def kernel(peers, ls_hbm, img, txt, grads, sums, ls, acc, X, S, A, lanes, stats, near_part, far_part, LR, AR,
           lsem, ssem, rsem, hop_ssem, hop_rsem, near_ssem, near_rsem, far_ssem, far_rsem, ar_ssem, ar_rsem, known):
    rows, width = img.shape[1], img.shape[2]
    piece = rows // PARTS
    b = lax.axis_index("blk")
    rep = lax.axis_index("rep")
    core = lax.rem(b, 2)
    other = 1 - core
    sib = b + 1 - 2 * core

    def ring(d):
        return (lax.rem(b + d + peers, peers), rep)

    step = (ring(2), ring(-2))
    sibling = (sib, rep)
    own = (txt, img)

    def remote(src, dst, s, r, d):
        return pltpu.make_async_remote_copy(
            src_ref=src, dst_ref=dst, send_sem=s, recv_sem=r, device_id=d, device_id_type=MESH)

    def signal(sem, d):
        pl.semaphore_signal(sem, inc=1, device_id=d, device_id_type=MESH)

    barrier = pltpu.get_barrier_semaphore()
    greeted = (step[0], step[1], sibling, (b, 1 - rep))
    for d in greeted:
        signal(barrier, d)
    loads = [pltpu.make_async_copy(own[p].at[0], X.at[p, pl.ds(0, rows)], lsem.at[p]) for p in range(2)]
    loads.append(pltpu.make_async_copy(ls_hbm, ls, lsem.at[2]))
    for load in loads:
        load.start()
    pl.semaphore_wait(barrier, len(greeted))

    def at(k, j):
        return pl.ds(pl.multiple_of(rows * k + j * piece, piece), piece)

    def arrived(p, k, j):
        here = X.at[p, at(k, j)]
        remote(here, here, ssem.at[0, 0], rsem.at[p, k, j], sibling).wait_recv()

    hop_piece = rows // HOP_PARTS

    def hop_at(k, i):
        return pl.ds(pl.multiple_of(rows * k + i * hop_piece, hop_piece), hop_piece)

    def hopped(p, far, i):
        here = X.at[p, hop_at(2 + 2 * far, i)]
        remote(here, here, hop_ssem.at[0, 0, 0], hop_rsem.at[p, far, i], sibling).wait_recv()

    def forward(i):
        for p in range(2):
            remote(X.at[p, hop_at(2, i)], X.at[p, hop_at(4, i)], hop_ssem.at[p, 1, i], hop_rsem.at[p, 1, i], step[p]).start()

    for i in range(HOP_PARTS):
        for p in range(2):
            remote(own[p].at[0, pl.ds(i * hop_piece, hop_piece)], X.at[p, hop_at(2, i)], hop_ssem.at[p, 0, i], hop_rsem.at[p, 0, i], step[p]).start()
    for load in loads:
        load.wait()
    for j in range(PARTS):
        remote(X.at[core, at(0, j)], X.at[core, at(1, j)], ssem.at[0, j], rsem.at[core, 1, j], sibling).start()

    scale2 = jnp.exp(ls[...]) * LOG2E
    lanes[0] = jnp.full(lanes.shape[1:], -jnp.inf, jnp.float32)
    lanes[1:3] = jnp.zeros((2,) + lanes.shape[1:], jnp.float32)
    acc[...] = jnp.zeros(acc.shape, jnp.float32)

    def logits(qp, qk, kp, first, n):
        return scale2 * lax.dot_general(
            X[qp, pl.ds(pl.multiple_of(qk * rows, TILE), rows)], X[kp, pl.ds(pl.multiple_of(first, TILE), n)],
            (((1,), (1,)), ((), ())), preferred_element_type=jnp.float32)

    def count(a, s):
        parts = [s[:, i:i + TILE] for i in range(0, s.shape[1], TILE)]
        old = lanes[0, a]
        top = functools.reduce(jnp.maximum, parts, old)
        fade = jnp.exp2(old - top)
        total, weighted = fade * lanes[1, a], fade * lanes[2, a]
        for part in parts:
            e = jnp.exp2(part - top)
            total = total + e
            weighted = weighted + e * part
        lanes[0, a], lanes[1, a], lanes[2, a] = top, total, weighted

    def score(p, first, n):
        s = logits(1 - p, 0, p, first, n)
        for i in range(n // TILE):
            S[p, first // TILE + i] = s[:, i * TILE:(i + 1) * TILE]
        count(p, s)

    @pl.loop(0, 2)
    def _(p):
        score(p, 0, rows)

    for j in range(PARTS):
        arrived(other, 1, j)
    score(other, rows, rows)

    def spread(r):
        for d in (4 << r, -(4 << r)):
            signal(known.at[r], ring(d))

    def learn(r):
        pl.semaphore_wait(known.at[r], 2)

    def near_scores(j):
        @pl.loop(0, 2)
        def _(p):
            score(p, 2 * rows + j * piece, piece)

        @pl.loop(0, 2)
        def _(i):
            p = lax.rem(core + i, 2)
            k = 1 + 2 * i

            @pl.when(jnp.logical_or(i == 1, j < PARTS - 1))
            def _():
                arrived(p, k, j)

            score(p, k * rows + j * piece, piece)

    @pl.loop(0, PARTS)
    def _(j):
        per = HOP_PARTS // PARTS
        for p in range(2):
            hopped(p, 0, j * per)

        @pl.when(j == 0)
        def _():
            spread(0)

        for i in range(1, per):
            for p in range(2):
                hopped(p, 0, j * per + i)
        for p in range(2):
            k = 3 - 2 * core if p == 0 else 1 + 2 * core
            remote(X.at[p, at(2, j)], X.at[p, at(k, j)], ssem.at[1 + p, j], rsem.at[p, k, j], sibling).start()

        @pl.when(j == 0)
        def _():
            forward(0)
            learn(0)
            spread(1)

        @pl.when(j == 1)
        def _():
            for i in (1, 2):
                forward(i)
            learn(1)
            spread(2)

        @pl.when(j < PARTS - 1)
        def _():
            near_scores(j)

    count(3, logits(core, 2, other, 2 * rows, rows))
    arrived(core, 1, PARTS - 1)

    @pl.loop(0, 2)
    def _(i):
        count(2, logits(other, 2, core, (1 + i) * rows, rows))

    def lay(a):
        top = jnp.max(lanes[0, a].T, axis=0, keepdims=True)
        fade = jnp.exp2(lanes[0, a].T - top)
        total = jnp.sum(fade * lanes[1, a].T, axis=0, keepdims=True)
        weighted = jnp.sum(fade * lanes[2, a].T, axis=0, keepdims=True)
        for j in range(PARTS):
            cols = slice(j * piece, (j + 1) * piece)
            stats[a, 0, j:j + 1] = top[:, cols]
            stats[a, 0, PARTS + j:PARTS + j + 1] = total[:, cols]
            stats[a, 1, j:j + 1] = weighted[:, cols]

    for i in range(2):
        lay(3 - i)
    for q in range(2):
        a = 3 - core if q == 0 else 2 + core
        far_part[q, 2] = stats[a]
        for k in (0, 1, 3, 4):
            there = ring(k - 2 if q == 0 else 2 - k)
            part = pl.ds(0, 2 if k == 0 else 1)
            remote(stats.at[a, part], far_part.at[q, k, part], far_ssem.at[q, k], far_rsem.at[q, k], there).start()
    near_scores(PARTS - 1)
    for p in range(2):
        lay(p)
        near_part[1 - p, 0] = stats[p]
    for q in range(2):
        for k in range(1, KEYS):
            part = pl.ds(0, 1)
            remote(stats.at[1 - q, part], near_part.at[q, k, part], near_ssem.at[q, k], near_rsem.at[q, k], ring(k if q == 0 else -k)).start()
    forward(3)
    forward(4)
    learn(2)
    spread(3)
    diag = jnp.zeros((), jnp.float32)
    one = (lax.broadcasted_iota(jnp.int32, (piece, piece), 0) == lax.broadcasted_iota(jnp.int32, (piece, piece), 1)).astype(jnp.float32)
    for j in range(PARTS):
        diag = diag + jnp.sum(S[0, j, pl.ds(j * piece, piece), :] * one)

    def merge(q, k):
        m1, m2 = near_part[q, k, 0, 0:PARTS], far_part[q, k, 0, 0:PARTS]
        l1, l2 = near_part[q, k, 0, PARTS:2 * PARTS], far_part[q, k, 0, PARTS:2 * PARTS]
        top = jnp.maximum(m1, m2)
        f1, f2 = jnp.exp2(m1 - top), jnp.exp2(m2 - top)
        total = f1 * l1 + f2 * l2
        half = top + jnp.log2(total) + 1.0
        for j in range(PARTS):
            LR[q, k, j, 0:1] = half[j:j + 1]
        return half, f1, f2, total

    def part_here(here, s, r):
        remote(here, here, s, r, sibling).wait_recv()

    lse_sum = -2.0 * rows
    pull = 0.0
    for q in range(2):
        part_here(far_part.at[q, 0], far_ssem.at[q, 0], far_rsem.at[q, 0])
        half, f1, f2, total = merge(q, 0)
        lse_sum = lse_sum + jnp.sum(half)
        pull = pull + jnp.sum((f1 * near_part[q, 0, 1, 0:PARTS] + f2 * far_part[q, 0, 1, 0:PARTS]) / total)
        for j in range(PARTS):
            A[1 - q, pl.ds(j * piece, piece)] = jnp.broadcast_to(half[j:j + 1], (TILE, piece)).T

    z, xl, y = lax.rem(b // 2, LINE), lax.rem(b // (2 * LINE), 2), b // (4 * LINE)
    x = 2 * rep + xl
    sizes = (LINE, LINE, 2)
    place = (z, 4 * y + x, core)

    def far_first(n):
        return sorted(range(n), key=lambda d: -min(d, n - d))

    def others(stage):
        if stage == 0:
            return [(b + 2 * (lax.rem(z + d, LINE) - z), rep) for d in far_first(LINE) if d]
        if stage == 1:
            found = []
            for dy, dx in sorted(((i, j) for i in range(4) for j in range(4)), key=lambda d: -sum(min(i, 4 - i) for i in d)):
                if dy or dx:
                    ny, nx = lax.rem(y + dy, 4), lax.rem(x + dx, 4)
                    found.append((4 * LINE * ny + 2 * LINE * lax.rem(nx, 2) + lax.rem(b, 2 * LINE), nx // 2))
            return found
        return [sibling]

    def share(stage, value):
        mine = AR.at[stage, place[stage]]
        mine[...] = value
        for d in others(stage):
            remote(mine, mine, ar_ssem.at[stage], ar_rsem.at[stage], d).start()

    def gather(stage):
        rest = AR.at[stage, pl.ds(0, sizes[stage] - 1)]
        remote(rest, rest, ar_ssem.at[stage], ar_rsem.at[stage], sibling).wait_recv()
        value = AR[stage, 0]
        for i in range(1, sizes[stage]):
            value = value + AR[stage, i]
        return value

    top_row = lax.broadcasted_iota(jnp.int32, (8, TILE), 0) == 0
    share(0, jnp.where(top_row, lse_sum - 2.0 * diag, 0.5 * pull - diag))
    forward(5)
    learn(3)
    spread(4)
    def halves(p, k, j, s):
        return jnp.exp2(s - A[p]) + jnp.exp2(s - LR[p, k, j, 0:1])

    for q in range(2):
        for k in range(1, KEYS):
            part = pl.ds(0, 1)
            part_here(near_part.at[q, k, part], near_ssem.at[q, k], near_rsem.at[q, k])
            if k != 2:
                part_here(far_part.at[q, k, part], far_ssem.at[q, k], far_rsem.at[q, k])
            merge(q, k)
    learn(4)
    spread(5)

    row_id = lax.broadcasted_iota(jnp.int32, (rows, piece), 0)
    col_id = lax.broadcasted_iota(jnp.int32, (rows, piece), 1)

    def near(p, k):
        hit = jnp.where(k == 0, 1.0, 0.0)
        g = [halves(p, k, j, S[p, k * PARTS + j]) - jnp.where(row_id == col_id + j * piece, hit, 0.0) for j in range(PARTS)]
        g = jnp.concatenate([t.astype(jnp.bfloat16) for t in g], axis=1)
        acc[p] += jnp.dot(g, X[p, pl.ds(pl.multiple_of(k * rows, TILE), rows)], preferred_element_type=jnp.float32)

    @pl.loop(0, 3)
    def _(k):
        near(0, k)
        near(1, k)

    near(other, 3)

    def far(j, *sides):
        keys, weights = [], []
        for p, slots in sides:
            x = [X[p, at(k, j)] for k in slots]
            keys.append(x[0] if len(x) == 1 else jnp.concatenate(x, axis=0))
        scores = [scale2 * lax.dot_general(X[1 - p, pl.ds(0, rows)], x, (((1,), (1,)), ((), ())), preferred_element_type=jnp.float32)
                  for (p, _), x in zip(sides, keys)]
        for (p, slots), s in zip(sides, scores):
            g = [halves(p, k, j, s[:, i * piece:(i + 1) * piece]).astype(jnp.bfloat16) for i, k in enumerate(slots)]
            weights.append(g[0] if len(g) == 1 else jnp.concatenate(g, axis=1))
        for (p, _), g, x in zip(sides, weights, keys):
            acc[p] += jnp.dot(g, x, preferred_element_type=jnp.float32)

    def far_here(p, j):
        per = HOP_PARTS // PARTS
        for i in range(per):
            hopped(p, 1, j * per + i)

    def far_relay(j):
        far_here(other, j)
        remote(X.at[other, at(4, j)], X.at[other, at(3, j)], ssem.at[3, j], rsem.at[other, 3, j], sibling).start()

    for j in range(PARTS - 1):
        far_relay(j)
        far_here(core, j)
        arrived(core, 3, j)
        far(j, (other, (4,)), (core, (3, 4)))
        if j == 0:
            learn(5)
            share(1, gather(0))
    far_relay(PARTS - 1)
    far(PARTS - 1, (other, (4,)))
    far_here(core, PARTS - 1)
    arrived(core, 3, PARTS - 1)
    far(PARTS - 1, (core, (3, 4)))
    share(2, gather(1))
    scale = jnp.exp(ls[...])
    for p in range(2):
        grads[p] = (scale * acc[p]).astype(jnp.bfloat16)
    unit = LN2 / (2 * peers * rows)
    sums[...] = gather(2) * jnp.where(top_row, 0.5 * unit, unit)

    for j in range(PARTS):
        for kind in range(4):
            here = X.at[0, at(0, 0)]
            remote(here, here, ssem.at[kind, j], rsem.at[0, 0, 0], sibling).wait_send()
    for i in range(HOP_PARTS):
        for p in range(2):
            for far_hop in range(2):
                here = X.at[0, hop_at(0, 0)]
                remote(here, here, hop_ssem.at[p, far_hop, i], hop_rsem.at[0, 0, 0], sibling).wait_send()
    for q in range(2):
        for k in range(KEYS):
            here = stats.at[0, pl.ds(0, 2 if k == 0 else 1)]
            if k != 2:
                remote(here, here, far_ssem.at[q, k], far_rsem.at[q, k], sibling).wait_send()
            if k != 0:
                remote(here, here, near_ssem.at[q, k], near_rsem.at[q, k], sibling).wait_send()
    for stage in range(3):
        rest = AR.at[stage, pl.ds(0, sizes[stage] - 1)]
        remote(rest, rest, ar_ssem.at[stage], ar_rsem.at[stage], sibling).wait_send()


def body(peers, images, texts, log_scale):
    _, rows, width = images.shape
    f32 = jnp.float32
    dma = pltpu.SemaphoreType.DMA
    vmem = pltpu.VMEM
    grads, sums = pl.pallas_call(
        functools.partial(kernel, peers),
        out_shape=(jax.ShapeDtypeStruct((2, rows, width), jnp.bfloat16), jax.ShapeDtypeStruct((8, TILE), f32)),
        in_specs=[pl.BlockSpec(memory_space=pl.ANY)] + [pl.BlockSpec(memory_space=pltpu.HBM)] * 2,
        out_specs=(pl.BlockSpec(memory_space=vmem),) * 2,
        scratch_shapes=[
            vmem((1, 1), f32),
            vmem((2, rows, width), f32),
            vmem((2, KEYS * rows, width), jnp.bfloat16),
            vmem((2, HOPS * PARTS, rows, rows // PARTS), f32),
            vmem((2, rows, TILE), f32),
            vmem((3, 4, rows, TILE), f32),
            vmem((4, 2, 8, TILE), f32),
            vmem((2, KEYS, 2, 8, TILE), f32),
            vmem((2, KEYS, 2, 8, TILE), f32),
            vmem((2, KEYS, PARTS, 8, TILE), f32),
            vmem((3, LINE, 8, TILE), f32),
            dma((3,)),
            dma((4, PARTS)),
            dma((2, KEYS, PARTS)),
            dma((2, 2, HOP_PARTS)),
            dma((2, 2, HOP_PARTS)),
            dma((2, KEYS)),
            dma((2, KEYS)),
            dma((2, KEYS)),
            dma((2, KEYS)),
            dma((3,)),
            dma((3,)),
            pltpu.SemaphoreType.REGULAR((6,)),
        ],
        compiler_params=pltpu.CompilerParams(
            collective_id=0, has_side_effects=True, vmem_limit_bytes=40 * 2**20),
        cost_estimate=pl.CostEstimate(
            flops=23 * 2 * rows * rows * width, bytes_accessed=4 * rows * width * 2, transcendentals=30 * rows * rows),
        name="band_clip",
    )(log_scale.reshape(1, 1), *(pltpu.with_memory_space_constraint(x, pltpu.HBM) for x in (images, texts)))
    return grads[0:1], grads[1:2], sums[0, 0], sums[1, 0]


def solution(mesh):
    placed = (P("rep", "blk", None), P("rep", "blk", None), P())
    return jax.shard_map(
        functools.partial(body, mesh.shape["blk"]),
        mesh=mesh,
        in_specs=placed,
        out_specs=(P("rep", "blk", None), P("rep", "blk", None), P(), P()),
        check_vma=False,
    )
```
